32 devices in a mesh: freq: 8 (over z, x), src: 2 (over y), rcv: 2 (over core).
Axes of the slice: x: 2, y: 2, z: 4, core: 2. Of those that a mesh axis runs over, the one named last changes fastest.
Arguments:
- traces: float32 [1024, 1024, 256], P(('src', 'freq'), 'rcv'), may hold values from -6 to 6
Outputs:
- multiples: float32 [2, 24, 1024, 1024], P(None, 'freq', 'src', 'rcv')
The draws below stay inside these ranges and needn't reach their ends.
All inputs are finite; a program needn't handle non-finite values.
Results may differ from the reference program's by a relative error of at most 0.000098.
Values sent between devices are 32-bit elements; how exact they have to be, the bound alone decides.
No kernel may reach another device: no remote copies, remote signals or barrier semaphores. Data moves between devices by JAX's collectives and lax.ppermute only.
A program may use at most 128 MiB of HBM per device.

```python
import math
import jax
import jax.numpy as jnp
from jax import lax

N = 1024
NT = 256
NF = 24


def levels(rng, dims, split, least, high):
    loudness, own = 1.0, jax.random.fold_in(rng, 6)
    for dim, parts in split:
        heights = jnp.exp(jax.random.uniform(jax.random.fold_in(own, dim), (parts,), jnp.float32, least / len(split), high / len(split)))
        loudness = loudness * jnp.repeat(heights, dims[dim] // parts).reshape([-1 if axis == dim else 1 for axis in range(len(dims))])
    return loudness


def centred(own_key, dims, spread, limit, pieces=(), kind=jnp.bfloat16):
    factor_of = levels(own_key, dims, pieces, -0.22, 0.18) if pieces else 1.0
    values = jax.random.normal(own_key, dims, jnp.float32) * spread * factor_of
    return jnp.minimum(jnp.maximum(values, -limit), limit).astype(kind)


def setup_inputs(seed: int = 0) -> dict:
    key_of = jax.random.split(jax.random.key(seed), 2)
    return {
        "traces": centred(key_of[0], (N, N, NT), 1.0, 6.0, ((0, 16), (1, 2)), jnp.float32),
    }


def dft_matrix(n_time, n_freq):
    times = jnp.arange(n_time, dtype=jnp.int32)
    bins = jnp.arange(n_freq, dtype=jnp.int32)
    phase = times[:, None] * bins[None, :] % n_time
    angle = phase.astype(jnp.float32) * (2.0 * math.pi / n_time)
    both = jnp.stack([jnp.cos(angle), -jnp.sin(angle)], axis=-1)
    return both.reshape(n_time, 2 * n_freq) * (1.0 / math.sqrt(n_time))

def partial_dot(left, right):
    return jnp.dot(left, right, precision=lax.Precision.HIGHEST, preferred_element_type=jnp.float32)

def reference(traces):
    dft_table = dft_matrix(NT, NF)
    block_size = N // 16
    grouped = traces.reshape(N // block_size, block_size * N, NT)

    def transform(source_block):
        return jnp.dot(source_block, dft_table, precision=lax.Precision.HIGHEST, preferred_element_type=jnp.float32)
    spectra = lax.map(transform, grouped).reshape(N, N, NF, 2)
    spectra_re = jnp.transpose(spectra[:, :, :, 0], (2, 0, 1))
    spectra_im = jnp.transpose(spectra[:, :, :, 1], (2, 0, 1))

    def multiply(pair):
        left_re, left_im = pair
        real_part = partial_dot(left_re, left_re) - partial_dot(left_im, left_im)
        imag_part = partial_dot(left_re, left_im) + partial_dot(left_im, left_re)
        return (real_part, imag_part)
    out_re, out_im = lax.map(multiply, (spectra_re, spectra_im))
    scale = -1.0 / math.sqrt(N)
    return jnp.stack([out_re, out_im]) * scale
```

```python
import functools
import math

import jax
import jax.numpy as jnp
from jax import lax
from jax.experimental import pallas as pl
from jax.experimental.pallas import tpu as pltpu
from jax.sharding import PartitionSpec as P

FPD = 3
WINDOW = 5
BF16 = jnp.bfloat16
F32 = jnp.float32


def split(x):
    high = x.astype(BF16)
    return high, (x - high.astype(F32)).astype(BF16)


def dft_rows(n_time, bins):
    times = jnp.arange(n_time, dtype=jnp.int32)
    phase = bins[:, None] * times[None, :] % n_time
    angle = phase.astype(F32) * (2.0 * math.pi / n_time)
    both = jnp.stack([jnp.cos(angle), -jnp.sin(angle)], axis=1)
    return both.reshape(-1, n_time) * (1.0 / math.sqrt(n_time))


def transform_kernel(sizes, table_ref, traces_ref, *refs):
    outs, scratch = refs[:-1], refs[-1]
    rows, step = sum(sizes), traces_ref.shape[0]
    contract = (((1,), (1,)), ((), ()))
    table_high, table_low = split(table_ref[...])
    table = jnp.concatenate([table_high, table_low])
    for s in range(step):
        high, low = split(traces_ref[s])
        both = lax.dot_general(table, high, contract, preferred_element_type=F32)
        rest = lax.dot_general(table_high, low, contract, preferred_element_type=F32)
        total = both[:rows] + (both[rows:] + rest)
        for lane in range(scratch.shape[0]):
            scratch[lane, pl.ds(s, rows, stride=step), :] = total[:, lane * 128 : (lane + 1) * 128]
    at = 0
    for size, out in zip(sizes, outs):
        for lane in range(scratch.shape[0]):
            block = scratch[lane, at * step : (at + size) * step, :]
            out[:, :, lane * 128 : (lane + 1) * 128] = block.reshape(size, step, 128)
        at += size


def transform(traces, table, sizes):
    n_src, n_rcv, n_time = traces.shape
    rows, step = sum(sizes), 8
    return pl.pallas_call(
        functools.partial(transform_kernel, sizes),
        grid=(n_src // step,),
        in_specs=[
            pl.BlockSpec((rows, n_time), lambda i: (0, 0)),
            pl.BlockSpec((step, n_rcv, n_time), lambda i: (i, 0, 0)),
        ],
        out_specs=[pl.BlockSpec((n, step, n_rcv), lambda i: (0, i, 0)) for n in sizes],
        out_shape=[jax.ShapeDtypeStruct((n, n_src, n_rcv), F32) for n in sizes],
        scratch_shapes=[pltpu.VMEM((n_rcv // 128, rows * step, 128), F32)],
        compiler_params=pltpu.CompilerParams(vmem_limit_bytes=48 << 20),
        cost_estimate=pl.CostEstimate(
            flops=6 * rows * n_src * n_rcv * n_time,
            bytes_accessed=4 * traces.size + 4 * rows * n_src * n_rcv,
            transcendentals=0,
        ),
    )(table, traces)


def product_kernel(scale, n_freq, n_src, n_rcv, place_ref, *refs):
    lefts = refs[: n_rcv * n_freq]
    rights = refs[n_rcv * n_freq : (n_rcv + n_src - 1) * n_freq]
    out, l_high, l_low, r_high, r_low = refs[-5:]
    freq, src, rcv = place_ref[0], place_ref[1], place_ref[2]
    _, height, width = lefts[0].shape
    rows = n_freq * height

    def put(high_ref, low_ref, top, left, block):
        high, low = split(block[...])
        where = (slice(None), pl.ds(pl.multiple_of(top, height), height), pl.ds(pl.multiple_of(left, 128), width))
        high_ref[where] = high
        low_ref[where] = low

    for peer in range(n_rcv):
        for d in range(n_freq):
            put(l_high, l_low, (freq ^ d) * height, (rcv ^ peer) * width, lefts[peer * n_freq + d])
    for peer in range(n_src):
        for d in range(n_freq):
            block = lefts[d] if peer == 0 else rights[(peer - 1) * n_freq + d]
            put(r_high, r_low, (src ^ peer) * rows + (freq ^ d) * height, 0, block)

    tile = min(256, rows)

    def dot(a, b):
        return jnp.dot(a, b, preferred_element_type=F32)

    def product(at, i, j):
        m = pl.ds(at, tile)
        return (
            dot(l_high[i, m, :], r_low[j])
            + dot(l_low[i, m, :], r_high[j])
            + dot(l_high[i, m, :], r_high[j])
        )

    for step in range(rows // tile):
        at = step * tile
        out[0, 0, pl.ds(at, tile), :] = scale * (product(at, 0, 0) - product(at, 1, 1))
        out[1, 0, pl.ds(at, tile), :] = scale * (product(at, 0, 1) + product(at, 1, 0))


def product(place, f, lefts, rights, done, mesh_sizes, scale):
    n_freq, n_src, n_rcv = mesh_sizes
    blocks = lefts + rights
    height, width = blocks[0][0].shape[1:]
    rows, inner = n_freq * height, n_src * n_freq * height

    def spec(at):
        return pl.BlockSpec((2, height, width), lambda i, place: (at, 0, 0))

    in_specs = [spec(at) for _, at in blocks]
    operands = [array for array, _ in blocks]
    alias = {}
    if done is not None:
        in_specs.append(pl.BlockSpec(memory_space=pl.ANY))
        operands.append(done)
        alias = {len(operands): 0}
    return pl.pallas_call(
        functools.partial(product_kernel, scale, n_freq, n_src, n_rcv),
        grid_spec=pltpu.PrefetchScalarGridSpec(
            num_scalar_prefetch=1,
            grid=(1,),
            in_specs=in_specs,
            out_specs=pl.BlockSpec((2, 1, rows, width), lambda i, place: (0, f, 0, 0)),
            scratch_shapes=[
                pltpu.VMEM((2, rows, inner), BF16),
                pltpu.VMEM((2, rows, inner), BF16),
                pltpu.VMEM((2, inner, width), BF16),
                pltpu.VMEM((2, inner, width), BF16),
            ],
        ),
        out_shape=jax.ShapeDtypeStruct((2, FPD, rows, width), F32),
        input_output_aliases=alias,
        compiler_params=pltpu.CompilerParams(vmem_limit_bytes=48 << 20),
        cost_estimate=pl.CostEstimate(
            flops=24 * rows * inner * width,
            bytes_accessed=4 * 2 * (rows * inner + inner * width + rows * width),
            transcendentals=0,
        ),
    )(place, *operands)


def per_device(traces):
    n_freq, n_src, n_rcv = (lax.axis_size(a) for a in ("freq", "src", "rcv"))
    freq = lax.axis_index("freq")
    place = jnp.stack([freq, lax.axis_index("src"), lax.axis_index("rcv")]).astype(jnp.int32)
    scale = -1.0 / math.sqrt(traces.shape[0] * n_freq * n_src)
    half = n_freq // 2

    pieces = [(d, tuple(range(FPD))) for d in range(half)]
    pieces += [(d, (f,)) for f in range(FPD) for d in range(half, n_freq)]
    bins = jnp.stack([(freq ^ d) * FPD + f for d, fs in pieces for f in fs])
    spectra = transform(traces, dft_rows(traces.shape[2], bins), [2 * len(fs) for _, fs in pieces])

    order = []

    def send(x, axis, d):
        if len(order) >= WINDOW:
            x, _ = lax.optimization_barrier((x, order[-WINDOW]))
        size = lax.axis_size(axis)
        y = lax.ppermute(x, axis, [(i, i ^ d) for i in range(size)])
        order.append(y)
        return y

    arrived, lefts, rights = {}, {}, {}

    def over_freq(p):
        d, _ = pieces[p]
        arrived[p] = send(spectra[p], "freq", d) if d else spectra[p]

    def onward(p):
        d, fs = pieces[p]
        peers = [arrived[p]] + [send(arrived[p], "rcv", e) for e in range(1, n_rcv)]
        others = [send(arrived[p], "src", e) for e in range(1, n_src)]
        for at, f in enumerate(fs):
            for e in range(n_rcv):
                lefts[f, e, d] = (peers[e], at)
            for e in range(1, n_src):
                rights[f, e, d] = (others[e - 1], at)

    far = list(range(half, len(pieces)))
    near = list(range(half))
    done = far[:2]
    for p in far[:2]:
        over_freq(p)
    over_freq(0)
    waiting = []
    queue = []
    nears = near[1:]
    fars = far[2:]
    onward_list = [0]
    for p in near[1:]:
        over_freq(p)
        onward(onward_list.pop(0))
        onward_list.append(p)
        if fars:
            q = fars.pop(0)
            over_freq(q)
            queue.append(q)
    onward_list += far[:2]
    onward_list += queue
    while onward_list:
        if fars:
            q = fars.pop(0)
            over_freq(q)
            onward_list.append(q)
        onward(onward_list.pop(0))

    out = None
    for f in range(FPD):
        left = [lefts[f, e, d] for e in range(n_rcv) for d in range(n_freq)]
        right = [rights[f, e, d] for e in range(1, n_src) for d in range(n_freq)]
        out = product(place, f, left, right, out, (n_freq, n_src, n_rcv), scale)
    return out


def solution(mesh):
    in_specs = (P(("src", "freq"), "rcv", None),)
    out_specs = P(None, "freq", "src", "rcv")
    return jax.shard_map(
        per_device, mesh=mesh, in_specs=in_specs, out_specs=out_specs, check_vma=False
    )
```

```python
import functools
import math

import jax
import jax.numpy as jnp
from jax import lax
from jax.experimental import pallas as pl
from jax.experimental.pallas import tpu as pltpu
from jax.sharding import PartitionSpec as P

FPD = 3
MIB = 1 << 20
EARLY = 2
BF16 = jnp.bfloat16
F32 = jnp.float32


def split(x):
    high = x.astype(BF16)
    return high, (x - high.astype(F32)).astype(BF16)


def dft_rows(n_time, bins):
    times = jnp.arange(n_time, dtype=jnp.int32)
    phase = bins[:, None] * times[None, :] % n_time
    angle = phase.astype(F32) * (2.0 * math.pi / n_time)
    both = jnp.stack([jnp.cos(angle), -jnp.sin(angle)], axis=1)
    return both.reshape(-1, n_time) * (1.0 / math.sqrt(n_time))


def transform_kernel(sizes, table_ref, traces_ref, *refs):
    outs, scratch = refs[:-1], refs[-1]
    rows, step = sum(sizes), traces_ref.shape[0]
    contract = (((1,), (1,)), ((), ()))
    table_high, table_low = split(table_ref[...])
    table = jnp.concatenate([table_high, table_low])
    for s in range(step):
        high, low = split(traces_ref[s])
        both = lax.dot_general(table, high, contract, preferred_element_type=F32)
        rest = lax.dot_general(table_high, low, contract, preferred_element_type=F32)
        total = both[:rows] + (both[rows:] + rest)
        for lane in range(scratch.shape[0]):
            scratch[lane, pl.ds(s, rows, stride=step), :] = total[:, lane * 128 : (lane + 1) * 128]
    at = 0
    for size, out in zip(sizes, outs):
        for lane in range(scratch.shape[0]):
            block = scratch[lane, at * step : (at + size) * step, :]
            out[:, :, lane * 128 : (lane + 1) * 128] = block.reshape(size, step, 128)
        at += size


def transform(traces, table, sizes):
    n_src, n_rcv, n_time = traces.shape
    rows, step = sum(sizes), 8
    return pl.pallas_call(
        functools.partial(transform_kernel, sizes),
        grid=(n_src // step,),
        in_specs=[
            pl.BlockSpec((rows, n_time), lambda i: (0, 0)),
            pl.BlockSpec((step, n_rcv, n_time), lambda i: (i, 0, 0)),
        ],
        out_specs=[pl.BlockSpec((n, step, n_rcv), lambda i: (0, i, 0)) for n in sizes],
        out_shape=[jax.ShapeDtypeStruct((n, n_src, n_rcv), F32) for n in sizes],
        scratch_shapes=[pltpu.VMEM((n_rcv // 128, rows * step, 128), F32)],
        compiler_params=pltpu.CompilerParams(vmem_limit_bytes=40 * MIB),
        cost_estimate=pl.CostEstimate(
            flops=6 * rows * n_src * n_rcv * n_time,
            bytes_accessed=4 * traces.size + 4 * rows * n_src * n_rcv,
            transcendentals=0,
        ),
    )(table, traces)


ANY = pl.BlockSpec(memory_space=pl.ANY)
CHEAP = pl.CostEstimate(flops=1, bytes_accessed=1, transcendentals=0)


def product_kernel(scale, f, natural, lefts_at, rights_at, sizes, n_in, place_ref, *refs):
    n_freq, n_src, n_rcv = sizes
    out = refs[n_in]
    left, right, l_high, l_low, r_high, r_low, result, sems, out_sems = refs[-9:]
    freq, src, rcv = place_ref[0], place_ref[1], place_ref[2]
    _, _, rows, width = left.shape
    height = rows // n_freq

    def fetch(target, blocks, n):
        copies = []
        for d, (array, first) in enumerate(blocks):
            top = d * height if natural else pl.multiple_of((freq ^ d) * height, height)
            copies.append(
                pltpu.make_async_copy(
                    refs[array].at[pl.ds(first, 2)], target.at[:, pl.ds(top, height)], sems.at[n + d]
                )
            )
            copies[-1].start()
        return copies

    copies = [fetch(left.at[e], lefts_at[e], e * n_freq) for e in range(n_rcv)]
    copies += [fetch(right.at[e], rights_at[e], (n_rcv + e) * n_freq) for e in range(n_src - 1)]

    for e in range(n_rcv):
        for copy in copies[e]:
            copy.wait()
        high, low = split(left[e])
        at = pl.ds(pl.multiple_of((rcv ^ e) * width, 128), width)
        l_high[:, :, at] = high
        l_low[:, :, at] = low
        if e == 0:
            at = pl.ds(pl.multiple_of(src * rows, rows), rows)
            r_high[:, at, :] = high
            r_low[:, at, :] = low
    for e in range(n_src - 1):
        for copy in copies[n_rcv + e]:
            copy.wait()
        high, low = split(right[e])
        at = pl.ds(pl.multiple_of((src ^ (e + 1)) * rows, rows), rows)
        r_high[:, at, :] = high
        r_low[:, at, :] = low

    tile = min(256, rows)

    def dot(a, b):
        return jnp.dot(a, b, preferred_element_type=F32)

    def part(m, i, j):
        return (
            dot(l_high[i, m, :], r_low[j])
            + dot(l_low[i, m, :], r_high[j])
            + dot(l_high[i, m, :], r_high[j])
        )

    copies = []
    for step in range(rows // tile):
        m = pl.ds(step * tile, tile)
        result[0, m, :] = scale * (part(m, 0, 0) - part(m, 1, 1))
        result[1, m, :] = scale * (part(m, 0, 1) + part(m, 1, 0))
        copies.append(pltpu.make_async_copy(result.at[:, m], out.at[:, f, m], out_sems.at[step]))
        copies[-1].start()
    for copy in copies:
        copy.wait()


def product(place, f, natural, lefts, rights, done, later, sizes, scale):
    n_freq, n_src, n_rcv = sizes
    height, width = lefts[0][0][0].shape[1:]
    rows, inner = n_freq * height, n_src * n_freq * height
    operands = []

    def place_of(blocks):
        found = []
        for array, first in blocks:
            known = [n for n, x in enumerate(operands) if x is array]
            if not known:
                operands.append(array)
            found.append((known[0] if known else len(operands) - 1, first))
        return found

    lefts_at, rights_at = [place_of(x) for x in lefts], [place_of(x) for x in rights]
    alias = {}
    shapes = [jax.ShapeDtypeStruct((2, FPD, rows, width), F32)]
    if done is not None:
        operands.append(done)
        alias[len(operands)] = 0
    for x in later:
        operands.append(x)
        alias[len(operands)] = len(shapes)
        shapes.append(jax.ShapeDtypeStruct(x.shape, x.dtype))
    return pl.pallas_call(
        functools.partial(product_kernel, scale, f, natural, lefts_at, rights_at, sizes, len(operands)),
        in_specs=[pl.BlockSpec(memory_space=pltpu.SMEM)] + [ANY] * len(operands),
        out_specs=[ANY] * len(shapes),
        out_shape=shapes,
        scratch_shapes=[
            pltpu.VMEM((n_rcv, 2, rows, width), F32),
            pltpu.VMEM((n_src - 1, 2, rows, width), F32),
            pltpu.VMEM((2, rows, inner), BF16),
            pltpu.VMEM((2, rows, inner), BF16),
            pltpu.VMEM((2, inner, width), BF16),
            pltpu.VMEM((2, inner, width), BF16),
            pltpu.VMEM((2, rows, width), F32),
            pltpu.SemaphoreType.DMA(((n_rcv + n_src - 1) * n_freq,)),
            pltpu.SemaphoreType.DMA((max(1, rows // 256),)),
        ],
        input_output_aliases=alias,
        compiler_params=pltpu.CompilerParams(vmem_limit_bytes=61 * MIB),
        cost_estimate=CHEAP
        if later
        else pl.CostEstimate(
            flops=24 * rows * inner * width,
            bytes_accessed=8 * (rows * inner + inner * width + rows * width),
            transcendentals=0,
        ),
    )(place, *operands)


def per_device(traces):
    n_freq, n_src, n_rcv = (lax.axis_size(a) for a in ("freq", "src", "rcv"))
    freq = lax.axis_index("freq")
    place = jnp.stack([freq, lax.axis_index("src"), lax.axis_index("rcv")]).astype(jnp.int32)
    scale = -1.0 / math.sqrt(traces.shape[0] * n_freq * n_src)
    half = n_freq // 2

    rest = FPD - 1
    sizes = (n_freq, n_src, n_rcv)

    pieces = [(d, tuple(range(1, FPD))) for d in range(half)]
    pieces += [(d, (f,)) for f in range(1, FPD) for d in range(half, n_freq)]
    bins = [jnp.arange(n_freq) * FPD] + [(freq ^ d) * FPD + jnp.array(fs) for d, fs in pieces]
    table = dft_rows(traces.shape[2], jnp.concatenate(bins))
    spectra = transform(traces, table, [2 * n_freq] + [2 * len(fs) for _, fs in pieces])
    whole, near, far = spectra[0], spectra[1 : half + 1], spectra[half + 1 :]

    def after(x, *others):
        return lax.optimization_barrier((x, *others))[0] if others else x

    def swap(x, axis, d, name):
        with jax.named_scope(name):
            return lax.ppermute(x, axis, [(i, i ^ d) for i in range(lax.axis_size(axis))])

    def to_src(x, name):
        return [swap(x, "src", e, name) for e in range(1, n_src)]

    def to_rcv(x, name):
        return [x] + [swap(x, "rcv", e, name) for e in range(1, n_rcv)]

    def every(x, first=0):
        return [(x, 2 * d) for d in range(n_freq)]

    first = lax.all_to_all(whole, "freq", split_axis=0, concat_axis=0, tiled=True)
    arrived, near_src = [near[0]], [to_src(near[0], "near_src_0")]

    def near_piece(d, *others):
        arrived.append(swap(after(near[d], *others), "freq", d, "near_freq_%d" % d))
        near_src.append(to_src(arrived[d], "near_src_%d" % d))

    for d in range(1, EARLY):
        near_piece(d)
    first_src = to_src(after(first, *[y for ys in near_src for y in ys]), "first_src")
    first_rcv = to_rcv(first, "first_rcv")
    for d in range(EARLY, half):
        near_piece(d, first)

    ready = [(0, True, [every(x) for x in first_rcv], [every(x) for x in first_src])]
    out = None
    before, ties = [first], [[]] * half
    for f in range(1, FPD):
        here, mine = [], list(far[(f - 1) * half : f * half])
        if f == FPD - 1:
            for done in ready[:-1]:
                out, mine[-1] = product(place, *done, out, [mine[-1]], sizes, scale)
        for i, x in enumerate(mine):
            here.append(swap(after(x, *before, *ties[i]), "freq", half + i, "far_freq_%d_%d" % (f, i)))
        far_src = [to_src(x, "far_src_%d_%d" % (f, i)) for i, x in enumerate(here)]
        own = [x[2 * (f - 1) : 2 * f] for x in arrived]
        x = jnp.concatenate(own + here)
        if f == FPD - 1:
            x = after(x, *[y for ys in far_src[: half // 2] for y in ys])
        gathered = to_rcv(x, "rcv_%d" % f)
        before = here + arrived[EARLY:] + first_src
        due = [y for ys in near_src[EARLY:] for y in ys] if f == 1 else []
        ties = [[] for _ in range(half)]
        for n, y in enumerate((due + [y for ys in far_src for y in ys])[: 2 * half - EARLY]):
            ties[min(1 + (n + 1) // 2, half - 1)].append(y)
        right = []
        for e in range(n_src - 1):
            right.append([(ys[e], 2 * (f - 1)) for ys in near_src] + [(ys[e], 0) for ys in far_src])
        ready.append((f, False, [every(x) for x in gathered], right))
    for done in ready[-2:]:
        out = product(place, *done, out, [], sizes, scale)[0]
    return out


def solution(mesh):
    in_specs = (P(("src", "freq"), "rcv", None),)
    out_specs = P(None, "freq", "src", "rcv")
    return jax.shard_map(
        per_device, mesh=mesh, in_specs=in_specs, out_specs=out_specs, check_vma=False
    )
```

```python
import functools
import math

import jax
import jax.numpy as jnp
from jax import lax
from jax.experimental import pallas as pl
from jax.experimental.pallas import tpu as pltpu
from jax.sharding import PartitionSpec as P

FPD = 3
MIB = 1 << 20
EARLY = 2
BF16 = jnp.bfloat16
F32 = jnp.float32


def split(x):
    high = x.astype(BF16)
    return high, (x - high.astype(F32)).astype(BF16)


def dft_rows(n_time, bins):
    times = jnp.arange(n_time, dtype=jnp.int32)
    phase = bins[:, None] * times[None, :] % n_time
    angle = phase.astype(F32) * (2.0 * math.pi / n_time)
    both = jnp.stack([jnp.cos(angle), -jnp.sin(angle)], axis=1)
    return both.reshape(-1, n_time) * (1.0 / math.sqrt(n_time))


def transform_kernel(sizes, table_ref, traces_ref, *refs):
    outs, scratch = refs[:-1], refs[-1]
    rows, step = sum(sizes), traces_ref.shape[0]
    contract = (((1,), (1,)), ((), ()))
    table_high, table_low = split(table_ref[...])
    table = jnp.concatenate([table_high, table_low])
    for s in range(step):
        high, low = split(traces_ref[s])
        both = lax.dot_general(table, high, contract, preferred_element_type=F32)
        rest = lax.dot_general(table_high, low, contract, preferred_element_type=F32)
        total = both[:rows] + (both[rows:] + rest)
        for lane in range(scratch.shape[0]):
            scratch[lane, pl.ds(s, rows, stride=step), :] = total[:, lane * 128 : (lane + 1) * 128]
    at = 0
    for size, out in zip(sizes, outs):
        for lane in range(scratch.shape[0]):
            block = scratch[lane, at * step : (at + size) * step, :]
            out[:, :, lane * 128 : (lane + 1) * 128] = block.reshape(size, step, 128)
        at += size


def transform(traces, table, sizes):
    n_src, n_rcv, n_time = traces.shape
    rows, step = sum(sizes), 8
    return pl.pallas_call(
        functools.partial(transform_kernel, sizes),
        grid=(n_src // step,),
        in_specs=[
            pl.BlockSpec((rows, n_time), lambda i: (0, 0)),
            pl.BlockSpec((step, n_rcv, n_time), lambda i: (i, 0, 0)),
        ],
        out_specs=[pl.BlockSpec((n, step, n_rcv), lambda i: (0, i, 0)) for n in sizes],
        out_shape=[jax.ShapeDtypeStruct((n, n_src, n_rcv), F32) for n in sizes],
        scratch_shapes=[pltpu.VMEM((n_rcv // 128, rows * step, 128), F32)],
        compiler_params=pltpu.CompilerParams(vmem_limit_bytes=32 * MIB),
        cost_estimate=pl.CostEstimate(
            flops=6 * rows * n_src * n_rcv * n_time,
            bytes_accessed=4 * traces.size + 4 * rows * n_src * n_rcv,
            transcendentals=0,
        ),
    )(table, traces)


ANY = pl.BlockSpec(memory_space=pl.ANY)
CHEAP = pl.CostEstimate(flops=1, bytes_accessed=1, transcendentals=0)


def product_kernel(scale, f, natural, lefts_at, rights_at, sizes, n_in, place_ref, *refs):
    n_freq, n_src, n_rcv = sizes
    out = refs[n_in]
    left, right, l_high, l_low, r_high, r_low, result, sems, out_sems = refs[-9:]
    freq, src, rcv = place_ref[0], place_ref[1], place_ref[2]
    _, _, rows, width = left.shape
    height = rows // n_freq

    def fetch(target, blocks, n):
        copies = []
        for d, (array, first) in enumerate(blocks):
            top = d * height if natural else pl.multiple_of((freq ^ d) * height, height)
            copies.append(
                pltpu.make_async_copy(
                    refs[array].at[pl.ds(first, 2)], target.at[:, pl.ds(top, height)], sems.at[n + d]
                )
            )
            copies[-1].start()
        return copies

    copies = [fetch(left.at[e], lefts_at[e], e * n_freq) for e in range(n_rcv)]
    copies += [fetch(right.at[e], rights_at[e], (n_rcv + e) * n_freq) for e in range(n_src - 1)]

    for e in range(n_rcv):
        for copy in copies[e]:
            copy.wait()
        high, low = split(left[e])
        at = pl.ds(pl.multiple_of((rcv ^ e) * width, 128), width)
        l_high[:, :, at] = high
        l_low[:, :, at] = low
        if e == 0:
            at = pl.ds(pl.multiple_of(src * rows, rows), rows)
            r_high[:, at, :] = high
            r_low[:, at, :] = low
    for e in range(n_src - 1):
        for copy in copies[n_rcv + e]:
            copy.wait()
        high, low = split(right[e])
        at = pl.ds(pl.multiple_of((src ^ (e + 1)) * rows, rows), rows)
        r_high[:, at, :] = high
        r_low[:, at, :] = low

    tile = min(256, rows)

    def dot(a, b):
        return jnp.dot(a, b, preferred_element_type=F32)

    def part(m, i, j):
        return (
            dot(l_high[i, m, :], r_low[j])
            + dot(l_low[i, m, :], r_high[j])
            + dot(l_high[i, m, :], r_high[j])
        )

    copies = []
    for step in range(rows // tile):
        m = pl.ds(step * tile, tile)
        result[0, m, :] = scale * (part(m, 0, 0) - part(m, 1, 1))
        result[1, m, :] = scale * (part(m, 0, 1) + part(m, 1, 0))
        copies.append(pltpu.make_async_copy(result.at[:, m], out.at[:, f, m], out_sems.at[step]))
        copies[-1].start()
    for copy in copies:
        copy.wait()


def product(place, f, natural, lefts, rights, done, later, sizes, scale):
    n_freq, n_src, n_rcv = sizes
    height, width = lefts[0][0][0].shape[1:]
    rows, inner = n_freq * height, n_src * n_freq * height
    operands = []

    def place_of(blocks):
        found = []
        for array, first in blocks:
            known = [n for n, x in enumerate(operands) if x is array]
            if not known:
                operands.append(array)
            found.append((known[0] if known else len(operands) - 1, first))
        return found

    lefts_at, rights_at = [place_of(x) for x in lefts], [place_of(x) for x in rights]
    alias = {}
    shapes = [jax.ShapeDtypeStruct((2, FPD, rows, width), F32)]
    if done is not None:
        operands.append(done)
        alias[len(operands)] = 0
    for x in later:
        operands.append(x)
        alias[len(operands)] = len(shapes)
        shapes.append(jax.ShapeDtypeStruct(x.shape, x.dtype))
    return pl.pallas_call(
        functools.partial(product_kernel, scale, f, natural, lefts_at, rights_at, sizes, len(operands)),
        in_specs=[pl.BlockSpec(memory_space=pltpu.SMEM)] + [ANY] * len(operands),
        out_specs=[ANY] * len(shapes),
        out_shape=shapes,
        scratch_shapes=[
            pltpu.VMEM((n_rcv, 2, rows, width), F32),
            pltpu.VMEM((n_src - 1, 2, rows, width), F32),
            pltpu.VMEM((2, rows, inner), BF16),
            pltpu.VMEM((2, rows, inner), BF16),
            pltpu.VMEM((2, inner, width), BF16),
            pltpu.VMEM((2, inner, width), BF16),
            pltpu.VMEM((2, rows, width), F32),
            pltpu.SemaphoreType.DMA(((n_rcv + n_src - 1) * n_freq,)),
            pltpu.SemaphoreType.DMA((max(1, rows // 256),)),
        ],
        input_output_aliases=alias,
        compiler_params=pltpu.CompilerParams(vmem_limit_bytes=61 * MIB),
        cost_estimate=CHEAP
        if later
        else pl.CostEstimate(
            flops=24 * rows * inner * width,
            bytes_accessed=8 * (rows * inner + inner * width + rows * width),
            transcendentals=0,
        ),
    )(place, *operands)


def per_device(traces):
    n_freq, n_src, n_rcv = (lax.axis_size(a) for a in ("freq", "src", "rcv"))
    freq = lax.axis_index("freq")
    place = jnp.stack([freq, lax.axis_index("src"), lax.axis_index("rcv")]).astype(jnp.int32)
    scale = -1.0 / math.sqrt(traces.shape[0] * n_freq * n_src)
    half = n_freq // 2

    rest = FPD - 1
    sizes = (n_freq, n_src, n_rcv)

    pieces = [(d, tuple(range(1, FPD))) for d in range(half)]
    pieces += [(d, (f,)) for f in range(1, FPD) for d in range(half, n_freq)]
    bins = [jnp.arange(n_freq) * FPD] + [(freq ^ d) * FPD + jnp.array(fs) for d, fs in pieces]
    table = dft_rows(traces.shape[2], jnp.concatenate(bins))
    spectra = transform(traces, table, [2 * n_freq] + [2 * len(fs) for _, fs in pieces])
    whole, near, far = spectra[0], spectra[1 : half + 1], spectra[half + 1 :]

    def after(x, *others):
        return lax.optimization_barrier((x, *others))[0] if others else x

    def swap(x, axis, d, name):
        with jax.named_scope(name):
            return lax.ppermute(x, axis, [(i, i ^ d) for i in range(lax.axis_size(axis))])

    def to_src(x, name):
        return [swap(x, "src", e, name) for e in range(1, n_src)]

    def to_rcv(x, name):
        return [x] + [swap(x, "rcv", e, name) for e in range(1, n_rcv)]

    def every(x, first=0):
        return [(x, 2 * d) for d in range(n_freq)]

    first = lax.all_to_all(whole, "freq", split_axis=0, concat_axis=0, tiled=True)
    arrived, near_src = [near[0]], [to_src(near[0], "near_src_0")]

    def near_piece(d, *others):
        arrived.append(swap(after(near[d], *others), "freq", d, "near_freq_%d" % d))
        near_src.append(to_src(arrived[d], "near_src_%d" % d))

    for d in range(1, EARLY):
        near_piece(d)
    first_src = to_src(after(first, *[y for ys in near_src for y in ys]), "first_src")
    for d in range(EARLY, half):
        near_piece(d, first)

    ready, out = [], None
    before, ties = [first], [[]] * half
    queue = [ys[-1] for ys in near_src[EARLY:]]
    started = {}

    def start(f, i, *others):
        x = after(far[(f - 1) * half + i], *others)
        started[f, i] = swap(x, "freq", half + i, "far_freq_%d_%d" % (f, i))
        return started[f, i]

    far = list(far)
    for f in range(1, FPD):
        if f == FPD - 1:
            first_rcv = [first] + to_rcv(after(first, *before), "first_rcv")[1:]
            ready.insert(0, (0, True, [every(x) for x in first_rcv], [every(x) for x in first_src]))
            for done in ready[:-1]:
                out, far[-1] = product(place, *done, out, [far[-1]], sizes, scale)
        here = [started[f, i] if (f, i) in started else start(f, i, *before, *ties[i]) for i in range(half)]
        before = here + arrived[EARLY:] + first_src
        lead = [start(f + 1, i, *before) for i in range(half // 2)] if f < FPD - 1 else []
        far_src = []
        for i, x in enumerate(here):
            held = queue[-2:-1] + lead[i : i + 1] if lead[i : i + 1] else []
            far_src.append(to_src(after(x, *held), "far_src_%d_%d" % (f, i)))
            queue.append(far_src[-1][-1])
        own = [x[2 * (f - 1) : 2 * f] for x in arrived]
        x = jnp.concatenate(own + here)
        if f == FPD - 1:
            x = after(x, *queue[:-half], *[y for ys in far_src[: half // 2] for y in ys])
        gathered = to_rcv(x, "rcv_%d" % f)
        ties = [[] for _ in range(half)]
        ties[half - 2] = queue[:1]
        ties[half - 1] = queue[1:]
        right = []
        for e in range(n_src - 1):
            right.append([(ys[e], 2 * (f - 1)) for ys in near_src] + [(ys[e], 0) for ys in far_src])
        ready.append((f, False, [every(x) for x in gathered], right))
    for done in ready[-2:]:
        out = product(place, *done, out, [], sizes, scale)[0]
    return out


def solution(mesh):
    in_specs = (P(("src", "freq"), "rcv", None),)
    out_specs = P(None, "freq", "src", "rcv")
    return jax.shard_map(
        per_device, mesh=mesh, in_specs=in_specs, out_specs=out_specs, check_vma=False
    )
```
